32 devices in a mesh: row: 4 (over y, x), col: 8 (over z, core).
Axes of the slice: x: 2, y: 2, z: 4, core: 2. Of those that a mesh axis runs over, the one named last changes fastest.
Arguments:
- velocity: float32 [3, 128, 384, 1024], P(None, 'col', 'row'), may hold values from -6 to 6
- x_operator: float32 [1024, 1024], replicated, may hold values from -0.1875 to 0.1875
- y_operator: float32 [384, 384], replicated, may hold values from -0.3125 to 0.3125
- z_operator: float32 [128, 128], replicated, may hold values from -0.5 to 0.5
- y_metric: float32 [384], replicated, may hold values from 0.5 to 4
Outputs:
- grads: bfloat16 [9, 128, 384, 1024], P(None, None, 'col', 'row')
The draws below stay inside these ranges and needn't reach their ends.
All inputs are finite; a program needn't handle non-finite values.
Results may differ from the reference program's by a relative error of at most 0.0095.
Values may be sent and summed in bfloat16 or wider, within the bound.
A program may use at most 192 MiB of HBM per device.

```python
import math
import jax
import jax.numpy as jnp
from jax import lax

NX = 1024
NY = 384
NZ = 128


def levels(rng, shape, cuts, low, largest):
    loudness, own = 1.0, jax.random.fold_in(rng, 6)
    for axis_at, blocks in cuts:
        heights = jnp.exp(jax.random.uniform(jax.random.fold_in(own, axis_at), (blocks,), jnp.float32, low / len(cuts), largest / len(cuts)))
        loudness = loudness * jnp.repeat(heights, shape[axis_at] // blocks).reshape([-1 if axis == axis_at else 1 for axis in range(len(shape))])
    return loudness


def scatter_about(key, extent, scale, reach, split=(), kind=jnp.bfloat16):
    values = jax.random.normal(key, extent, jnp.float32) * scale
    if len(split) > 0:
        values = levels(key, extent, split, -0.22, 0.18) * values
    return jnp.clip(values, min=-reach, max=reach).astype(kind)


def setup_inputs(seed: int = 0) -> dict:
    key_of = jax.random.split(jax.random.key(seed), 6)
    return {
        "velocity": scatter_about(key_of[0], (3, NZ, NY, NX), 1.0, 6.0, ((1, 8), (2, 4)), jnp.float32),
        "x_operator": scatter_about(key_of[1], (NX, NX), NX ** -0.5, 0.1875, (), jnp.float32),
        "y_operator": scatter_about(key_of[2], (NY, NY), NY ** -0.5, 0.3125, (), jnp.float32),
        "z_operator": scatter_about(key_of[3], (NZ, NZ), NZ ** -0.5, 0.5, (), jnp.float32),
        "y_metric": jnp.clip(jnp.exp(jax.random.uniform(key_of[4], (NY,), jnp.float32, math.log(0.5), math.log(4.0))), 0.5, 4.0),
    }


HIGHEST = lax.Precision.HIGHEST


def reference(velocity, x_operator, y_operator, z_operator, y_metric):
    pieces = []
    for component in range(3):
        single = velocity[component]
        along_x = jnp.einsum('zyx,xw->zyw', single, x_operator, precision=HIGHEST)
        along_y = jnp.einsum('zyx,yw->zwx', single, y_operator, precision=HIGHEST) * y_metric[None, :, None]
        along_z = jnp.einsum('zyx,zw->wyx', single, z_operator, precision=HIGHEST)
        for derived in (along_x, along_y, along_z):
            pieces.append(derived.astype(jnp.bfloat16))
    return jnp.stack(pieces, axis=0)
```

```python
import functools

import jax
import jax.numpy as jnp
from jax import lax
from jax.experimental import pallas as pl
from jax.experimental.pallas import tpu as pltpu
from jax.sharding import PartitionSpec as P

MESH = pl.DeviceIdType.MESH
HALVES = 2


def kernel(
    rows, cols, halves, yop_ref, xop_ref, v_ref, vz_ref, gx_ref, gy_ref,
    ypen, ay, xpen, ax,
    row_v_s, row_v_r, col_v_s, col_v_r, col_y_s, col_y_r, row_f_s, row_f_r, row_x_s, row_x_r, own_sem,
):
    r, c = lax.axis_index("row"), lax.axis_index("col")
    k = cols // rows
    chunks, _, zh, yc, xb = ypen.shape
    ny = cols * yc

    barrier = pltpu.get_barrier_semaphore()
    for d in range(1, rows):
        pl.semaphore_signal(barrier, inc=1, device_id=(lax.rem(r + d, rows), c), device_id_type=MESH)
    for d in range(1, cols):
        pl.semaphore_signal(barrier, inc=1, device_id=(r, lax.rem(c + d, cols)), device_id_type=MESH)
    pl.semaphore_wait(barrier, rows + cols - 2)

    def place(q):
        return q // halves, pl.ds((q % halves) * zh, zh)

    def remote(src, dst, send, recv, target):
        return pltpu.make_async_remote_copy(
            src_ref=src, dst_ref=dst, send_sem=send, recv_sem=recv, device_id=target, device_id_type=MESH
        )

    def row_v(q):
        comp, zs = place(q)
        def src(t):
            return v_ref.at[comp, :, zs, :, pl.ds(pl.multiple_of(t * xb, 128), xb)]
        dst = ypen.at[q, pl.ds(r * k, k)]
        others = []
        for d in range(1, rows):
            t = lax.rem(r + d, rows)
            others.append(remote(src(t), dst, row_v_s.at[q, d - 1], row_v_r.at[q, d - 1], (t, c)))
        return others, pltpu.make_async_copy(src(r), dst, own_sem.at[0, q])

    def col_family(q, source, result, send, recv, own):
        comp, zs = place(q)
        dst = result.at[comp, c, zs]
        others = []
        for d in range(1, cols):
            t = lax.rem(c + d, cols)
            others.append(remote(source.at[q, t], dst, send.at[q, d - 1], recv.at[q, d - 1], (r, t)))
        return others, pltpu.make_async_copy(source.at[q, c], dst, own_sem.at[own, q])

    def col_v(q):
        return col_family(q, ypen, vz_ref, col_v_s, col_v_r, 1)

    def col_y(q):
        return col_family(q, ay, gy_ref, col_y_s, col_y_r, 2)

    def row_f(q):
        comp, zs = place(q)
        def src(t):
            return vz_ref.at[comp, pl.ds(t * k, k), zs]
        dst = xpen.at[q, r]
        others = []
        for d in range(1, rows):
            t = lax.rem(r + d, rows)
            others.append(remote(src(t), dst, row_f_s.at[q, d - 1], row_f_r.at[q, d - 1], (t, c)))
        return others, pltpu.make_async_copy(src(r), dst, own_sem.at[3, q])

    def row_x(q):
        comp, zs = place(q)
        dst = gx_ref.at[comp, pl.ds(r * k, k), zs]
        others = []
        for d in range(1, rows):
            t = lax.rem(r + d, rows)
            others.append(remote(ax.at[q, t], dst, row_x_s.at[q, d - 1], row_x_r.at[q, d - 1], (t, c)))
        return others, pltpu.make_async_copy(ax.at[q, r], dst, own_sem.at[4, q])

    def start(family, q):
        others, own = family(q)
        for copy in others:
            copy.start()
        own.start()

    def arrived(family, q):
        others, own = family(q)
        for copy in others:
            copy.wait_recv()
        own.wait()

    def sent(family, q):
        for copy in family(q)[0]:
            copy.wait_send()

    def flat(x, width):
        if yc % 16:
            return x.astype(jnp.float32).reshape(-1, width).astype(x.dtype)
        return x.reshape(-1, width)

    def along_y(q):
        @pl.loop(0, zh)
        def _(z):
            field = flat(ypen[q, :, z], xb)
            product = jnp.dot(yop_ref[...], field, preferred_element_type=jnp.float32)
            ay[q, :, z] = product.reshape(cols, yc, xb).astype(ay.dtype)

    def along_x(q):
        for part in range(k):
            field = jnp.concatenate([flat(xpen[q, j, part], xb) for j in range(rows)], axis=1)

            @pl.loop(0, rows)
            def _(w):
                product = jnp.dot(field, xop_ref[w], preferred_element_type=jnp.float32)
                ax[q, w, part] = product.reshape(zh, yc, xb).astype(ax.dtype)

    @pl.loop(0, chunks)
    def _(q):
        start(row_v, q)

    @pl.loop(0, chunks)
    def _(q):
        arrived(row_v, q)
        start(col_v, q)
        along_y(q)

    def finish_x(q):
        arrived(row_f, q)
        along_x(q)
        start(row_x, q)

    @pl.loop(0, chunks)
    def _(q):
        arrived(col_v, q)
        start(row_f, q)
        start(col_y, q)

        @pl.when(q > 0)
        def _():
            finish_x(q - 1)

    finish_x(chunks - 1)

    @pl.loop(0, chunks)
    def _(q):
        arrived(row_x, q)
        arrived(col_y, q)
        for family in (row_v, col_v, col_y, row_f, row_x):
            sent(family, q)


def shards(rows, cols, velocity, x_operator, y_operator, z_operator, y_metric):
    bf16 = jnp.bfloat16
    comps, zb, yb, nx = velocity.shape
    k = cols // rows
    yc, xb, ny = yb // k, nx // rows, yb * rows
    halves = HALVES
    zh, chunks = zb // halves, comps * halves

    v = velocity.astype(bf16).reshape(comps, zb, k, yc, nx).transpose(0, 2, 1, 3, 4)
    yop = (y_operator * y_metric[None, :]).T.astype(bf16)
    xop = x_operator.astype(bf16).reshape(nx, rows, xb).transpose(1, 0, 2)

    final = jax.ShapeDtypeStruct((comps, cols, zb, yc, xb), bf16)
    pencils = pltpu.VMEM((chunks, cols, zh, yc, xb), bf16)
    blocks = pltpu.VMEM((chunks, rows, k, zh, yc, xb), bf16)
    row_sem = pltpu.SemaphoreType.DMA((chunks, rows - 1))
    col_sem = pltpu.SemaphoreType.DMA((chunks, cols - 1))
    work = comps * zb * yb * nx
    vz, gx, gy = pl.pallas_call(
        functools.partial(kernel, rows, cols, halves),
        out_shape=[final] * 3,
        in_specs=[pl.BlockSpec(memory_space=pltpu.VMEM)] * 2 + [pl.BlockSpec(memory_space=pl.ANY)],
        out_specs=[pl.BlockSpec(memory_space=pl.ANY)] * 3,
        scratch_shapes=[
            pencils, pencils, blocks, blocks,
            row_sem, row_sem, col_sem, col_sem, col_sem, col_sem, row_sem, row_sem, row_sem, row_sem,
            pltpu.SemaphoreType.DMA((5, chunks)),
        ],
        cost_estimate=pl.CostEstimate(flops=2 * work * (nx + ny), bytes_accessed=10 * work, transcendentals=0),
        compiler_params=pltpu.CompilerParams(
            collective_id=0, has_side_effects=True, vmem_limit_bytes=56 * 2**20
        ),
    )(yop, xop, v)

    vz, gx, gy = (a.reshape(comps, cols * zb, yc, xb) for a in (vz, gx, gy))
    gz = jnp.einsum(
        "czyx,zw->cwyx", vz, z_operator.astype(bf16), preferred_element_type=jnp.float32
    ).astype(bf16)
    return jnp.stack([gx, gy, gz], axis=1).reshape(3 * comps, cols * zb, yc, xb)


def solution(mesh):
    return jax.shard_map(
        functools.partial(shards, mesh.shape["row"], mesh.shape["col"]),
        mesh=mesh,
        in_specs=(P(None, "col", "row", None), P(), P(), P(), P()),
        out_specs=P(None, None, "col", "row"),
        check_vma=False,
    )
```

```python
import functools

import jax
import jax.numpy as jnp
from jax import lax
from jax.experimental import pallas as pl
from jax.experimental.pallas import tpu as pltpu
from jax.sharding import PartitionSpec as P

MESH = pl.DeviceIdType.MESH
HALVES = 2


def kernel(
    rows, cols, halves, v_ref, yop_ref, metric_ref, zop_ref, xop_ref, vz_ref, g_ref,
    ypen, ay, xpen, blocks, stage, yop, kron,
    row_v_s, row_v_r, col_v_s, col_v_r, col_y_s, col_y_r, row_f_s, row_f_r, row_x_s, row_x_r, own_sem, stage_sem,
):
    r, c = lax.axis_index("row"), lax.axis_index("col")
    chunks, _, k, zh, yc, xb = ypen.shape
    zb, nz = zh * halves, zh * halves * cols
    group = 16 if yc % 16 == 0 else 8

    def place(q):
        return q // halves, pl.ds((q % halves) * zh, zh)

    def load(q):
        comp, zs = place(q)
        return pltpu.make_async_copy(v_ref.at[comp, zs], stage.at[q % 2], stage_sem.at[q % 2])

    load(0).start()
    load(1).start()

    barrier = pltpu.get_barrier_semaphore()
    for d in range(1, rows):
        pl.semaphore_signal(barrier, inc=1, device_id=(lax.rem(r + d, rows), c), device_id_type=MESH)
    for d in range(1, cols):
        pl.semaphore_signal(barrier, inc=1, device_id=(r, lax.rem(c + d, cols)), device_id_type=MESH)
    pl.semaphore_wait(barrier, rows + cols - 2)

    def remote(src, dst, send, recv, target):
        return pltpu.make_async_remote_copy(
            src_ref=src, dst_ref=dst, send_sem=send, recv_sem=recv, device_id=target, device_id_type=MESH
        )

    def row_family(q, source, dst, send, recv, own):
        others = []
        for d in range(1, rows):
            t = lax.rem(r + d, rows)
            others.append(remote(source(t), dst, send.at[q, d - 1], recv.at[q, d - 1], (t, c)))
        return others, pltpu.make_async_copy(source(r), dst, own_sem.at[own, q])

    def col_family(q, source, dst, send, recv, own):
        others = []
        for d in range(1, cols):
            t = lax.rem(c + d, cols)
            others.append(remote(source(t), dst, send.at[q, d - 1], recv.at[q, d - 1], (r, t)))
        return others, pltpu.make_async_copy(source(c), dst, own_sem.at[own, q])

    def row_v(q):
        return row_family(q, lambda t: blocks.at[q, t], ypen.at[q, r], row_v_s, row_v_r, 0)

    def col_v(q):
        comp, zs = place(q)
        dst = vz_ref.at[comp, c // k, c % k, zs]
        return col_family(q, lambda t: ypen.at[q, t // k, t % k], dst, col_v_s, col_v_r, 1)

    def col_y(q):
        comp, zs = place(q)
        dst = g_ref.at[comp, 1, c // k, c % k, zs]
        return col_family(q, lambda t: ay.at[q, t // k, t % k], dst, col_y_s, col_y_r, 2)

    def row_f(q):
        comp, zs = place(q)
        return row_family(q, lambda t: vz_ref.at[comp, t, :, zs], xpen.at[q, r], row_f_s, row_f_r, 3)

    def row_x(q):
        comp, zs = place(q)
        return row_family(q, lambda t: blocks.at[q, t], g_ref.at[comp, 0, r, :, zs], row_x_s, row_x_r, 4)

    def field_in(q):
        comp, zs = place(q)
        return pltpu.make_async_copy(vz_ref.at[comp, :, :, zs], ypen.at[q], own_sem.at[5, q])

    def along_z_out(q):
        comp, zs = place(q)
        return pltpu.make_async_copy(xpen.at[q], g_ref.at[comp, 2, :, :, zs], own_sem.at[6, q])

    def start(family, q):
        others, own = family(q)
        for copy in others:
            copy.start()
        own.start()

    def arrived(family, q):
        others, own = family(q)
        for copy in others:
            copy.wait_recv()
        own.wait()

    def sent(family, q):
        for copy in family(q)[0]:
            copy.wait_send()

    def flat(x, width):
        if yc % 16:
            return x.astype(jnp.float32).reshape(-1, width).astype(x.dtype)
        return x.reshape(-1, width)

    def cast(q):
        @pl.loop(0, zh)
        def _(z):
            for part in range(k):
                for w in range(rows):
                    field = stage[q % 2, z, pl.ds(part * yc, yc), pl.ds(w * xb, xb)]
                    blocks[q, w, part, z] = field.astype(blocks.dtype)

    def along_y(q):
        @pl.loop(0, zh)
        def _(z):
            field = flat(ypen[q, :, :, z], xb)
            product = jnp.dot(yop[...], field, preferred_element_type=jnp.float32)
            ay[q, :, :, z] = product.reshape(rows, k, yc, xb).astype(ay.dtype)

    def along_x(q):
        field = jnp.concatenate([flat(xpen[q, j], xb) for j in range(rows)], axis=1)

        @pl.loop(0, rows)
        def _(w):
            operator = xop_ref[:, pl.ds(pl.multiple_of(w * xb, 128), xb)]
            product = jnp.dot(field, operator, preferred_element_type=jnp.float32)
            blocks[q, w] = product.reshape(k, zh, yc, xb).astype(blocks.dtype)

    def z_of(n):
        half, block = n // (nz // halves * group), n // (zh * group) % cols
        return block * zb + half * zh + n // group % zh

    def make_kron():
        wide, tall = nz // halves * group, zh * group * k

        @pl.loop(0, halves * rows)
        def _(m):
            at = lax.broadcasted_iota(jnp.int32, (tall, nz), 0) + m * tall
            pick = jnp.where(z_of(at) == lax.broadcasted_iota(jnp.int32, (tall, nz), 1), 1.0, 0.0)
            line = lax.dot_general(
                pick.astype(kron.dtype), zop_ref[...].astype(kron.dtype), (((1,), (1,)), ((), ())),
                preferred_element_type=jnp.float32,
            ).astype(kron.dtype)
            for h in range(halves):
                across = lax.broadcasted_iota(jnp.int32, (nz, wide), 1) + h * wide
                spread = jnp.where(z_of(across) == lax.broadcasted_iota(jnp.int32, (nz, wide), 0), 1.0, 0.0)
                full = jnp.dot(line, spread.astype(kron.dtype), preferred_element_type=jnp.float32)
                down = lax.broadcasted_iota(jnp.int32, (tall, wide), 0) % group
                same = down == lax.broadcasted_iota(jnp.int32, (tall, wide), 1) % group
                kron[h, pl.ds(m * tall, tall)] = jnp.where(same, full, 0.0).astype(kron.dtype)

    def along_z(comp):
        tall = zh * group * k

        @pl.loop(0, halves * rows)
        def _(m):
            lines = []
            for g in range(yc // group):
                total = None
                for h in range(halves):
                    if yc % 16:
                        field = ypen[comp * halves + h].astype(jnp.float32)[:, :, :, g * group:(g + 1) * group]
                    else:
                        field = ypen[comp * halves + h, :, :, :, pl.ds(g * group, group)]
                    field = field.reshape(-1, xb).astype(kron.dtype)
                    part = jnp.dot(kron[h, pl.ds(m * tall, tall)], field, preferred_element_type=jnp.float32)
                    total = part if total is None else total + part
                lines.append(total.reshape(k, zh, group, xb))
            q = comp * halves + m // rows
            if yc % 16:
                xpen[q, m % rows] = jnp.concatenate(lines, axis=2).astype(xpen.dtype)
            else:
                for g, line in enumerate(lines):
                    xpen[q, m % rows, :, :, pl.ds(g * group, group)] = line.astype(xpen.dtype)

    @pl.loop(0, chunks)
    def _(q):
        load(q).wait()
        cast(q)

        @pl.when(q + 2 < chunks)
        def _():
            load(q + 2).start()

        start(row_v, q)

    yop[...] = (yop_ref[...] * metric_ref[...]).T.astype(yop.dtype)

    @pl.loop(0, chunks)
    def _(q):
        arrived(row_v, q)
        start(col_v, q)
        along_y(q)

    make_kron()

    def finish_x(q):
        sent(row_v, q)
        arrived(row_f, q)
        along_x(q)
        start(row_x, q)

    @pl.loop(0, chunks)
    def _(q):
        arrived(col_v, q)
        start(row_f, q)
        start(col_y, q)

        @pl.when(q > 0)
        def _():
            finish_x(q - 1)

    finish_x(chunks - 1)

    @pl.loop(0, chunks)
    def _(q):
        sent(col_v, q)
        field_in(q).start()

    @pl.loop(0, chunks // halves)
    def _(comp):
        for h in range(halves):
            field_in(comp * halves + h).wait()
        along_z(comp)
        for h in range(halves):
            along_z_out(comp * halves + h).start()

    @pl.loop(0, chunks)
    def _(q):
        arrived(row_x, q)
        arrived(col_y, q)
        along_z_out(q).wait()
        for family in (col_y, row_f, row_x):
            sent(family, q)


def shards(rows, cols, velocity, x_operator, y_operator, z_operator, y_metric):
    bf16 = jnp.bfloat16
    comps, zb, yb, nx = velocity.shape
    k = cols // rows
    yc, xb, ny, nz = yb // k, nx // rows, yb * rows, zb * cols
    halves = HALVES
    zh, chunks = zb // halves, comps * halves
    group = 16 if yc % 16 == 0 else 8

    buffer = pltpu.VMEM((chunks, rows, k, zh, yc, xb), bf16)
    row_sem = pltpu.SemaphoreType.DMA((chunks, rows - 1))
    col_sem = pltpu.SemaphoreType.DMA((chunks, cols - 1))
    work = comps * zb * yb * nx
    _, grads = pl.pallas_call(
        functools.partial(kernel, rows, cols, halves),
        out_shape=[
            jax.ShapeDtypeStruct((comps, rows, k, zb, yc, xb), bf16),
            jax.ShapeDtypeStruct((comps, 3, rows, k, zb, yc, xb), bf16),
        ],
        in_specs=[pl.BlockSpec(memory_space=pl.ANY)] + [pl.BlockSpec(memory_space=pltpu.VMEM)] * 4,
        out_specs=[pl.BlockSpec(memory_space=pl.ANY)] * 2,
        scratch_shapes=[
            buffer, buffer, buffer, buffer,
            pltpu.VMEM((2, zh, yb, nx), jnp.float32),
            pltpu.VMEM((ny, ny), bf16),
            pltpu.VMEM((halves, nz * group, nz // halves * group), bf16),
            row_sem, row_sem, col_sem, col_sem, col_sem, col_sem, row_sem, row_sem, row_sem, row_sem,
            pltpu.SemaphoreType.DMA((7, chunks)),
            pltpu.SemaphoreType.DMA((2,)),
        ],
        cost_estimate=pl.CostEstimate(
            flops=2 * work * (nx + ny + nz * group), bytes_accessed=14 * work, transcendentals=0
        ),
        compiler_params=pltpu.CompilerParams(
            collective_id=0, has_side_effects=True, vmem_limit_bytes=61 * 2**20
        ),
    )(velocity, y_operator, y_metric[None, :], z_operator, x_operator.astype(bf16))
    return grads.reshape(3 * comps, nz, yc, xb)


def solution(mesh):
    return jax.shard_map(
        functools.partial(shards, mesh.shape["row"], mesh.shape["col"]),
        mesh=mesh,
        in_specs=(P(None, "col", "row", None), P(), P(), P(), P()),
        out_specs=P(None, None, "col", "row"),
        check_vma=False,
    )
```

```python
import functools

import jax
import jax.numpy as jnp
from jax import lax
from jax.experimental import pallas as pl
from jax.experimental.pallas import tpu as pltpu
from jax.sharding import PartitionSpec as P

MESH = pl.DeviceIdType.MESH
PARTS = 4


def kernel(
    rows, cols, parts, v_ref, xop_ref, yop_ref, metric_ref, zop_ref, vz_ref, g_ref,
    ypen, ay, xpen, blocks, stage, xop_in, yop_in, xop, yop, kron,
    row_v_s, row_v_r, col_v_s, col_v_r, col_y_s, col_y_r, row_f_s, row_f_r, row_x_s, row_x_r, own_sem, stage_sem,
):
    r, c = lax.axis_index("row"), lax.axis_index("col")
    chunks, _, k, zh, yc, xb = ypen.shape
    zb, nz = zh * parts, zh * parts * cols
    group = 16 if yc % 16 == 0 else 8

    def place(q):
        return q // parts, pl.ds((q % parts) * zh, zh)

    def load(q):
        comp, zs = place(q)
        return pltpu.make_async_copy(v_ref.at[comp, zs], stage.at[q % 2], stage_sem.at[q % 2])

    def load_operators():
        return [
            pltpu.make_async_copy(yop_ref, yop_in, stage_sem.at[2]),
            pltpu.make_async_copy(xop_ref, xop_in, stage_sem.at[3]),
        ]

    load(0).start()
    load(1).start()
    for copy in load_operators():
        copy.start()

    barrier = pltpu.get_barrier_semaphore()
    for d in range(1, rows):
        pl.semaphore_signal(barrier, inc=1, device_id=(lax.rem(r + d, rows), c), device_id_type=MESH)
    for d in range(1, cols):
        pl.semaphore_signal(barrier, inc=1, device_id=(r, lax.rem(c + d, cols)), device_id_type=MESH)
    pl.semaphore_wait(barrier, rows + cols - 2)

    def remote(src, dst, send, recv, target):
        return pltpu.make_async_remote_copy(
            src_ref=src, dst_ref=dst, send_sem=send, recv_sem=recv, device_id=target, device_id_type=MESH
        )

    def row_family(q, source, dst, send, recv, own):
        others = []
        for d in range(1, rows):
            t = lax.rem(r + d, rows)
            others.append(remote(source(t), dst, send.at[q, d - 1], recv.at[q, d - 1], (t, c)))
        return others, pltpu.make_async_copy(source(r), dst, own_sem.at[own, q])

    def col_family(q, source, dst, send, recv, own):
        others = []
        for d in range(1, cols):
            t = lax.rem(c + d, cols)
            others.append(remote(source(t), dst, send.at[q, d - 1], recv.at[q, d - 1], (r, t)))
        return others, pltpu.make_async_copy(source(c), dst, own_sem.at[own, q])

    def row_v(q):
        return row_family(q, lambda t: blocks.at[q, t], ypen.at[q, r], row_v_s, row_v_r, 0)

    def col_v(q):
        comp, zs = place(q)
        dst = vz_ref.at[comp, c // k, c % k, zs]
        return col_family(q, lambda t: ypen.at[q, t // k, t % k], dst, col_v_s, col_v_r, 1)

    def col_y(q):
        comp, zs = place(q)
        dst = g_ref.at[comp, 1, c // k, c % k, zs]
        return col_family(q, lambda t: ay.at[q, t // k, t % k], dst, col_y_s, col_y_r, 2)

    def row_f(q):
        comp, zs = place(q)
        return row_family(q, lambda t: vz_ref.at[comp, t, :, zs], xpen.at[q, r], row_f_s, row_f_r, 3)

    def row_x(q):
        comp, zs = place(q)
        return row_family(q, lambda t: blocks.at[q, t], g_ref.at[comp, 0, r, :, zs], row_x_s, row_x_r, 4)

    def field_in(q):
        comp, zs = place(q)
        return pltpu.make_async_copy(vz_ref.at[comp, :, :, zs], ypen.at[q], own_sem.at[5, q])

    def along_z_out(q):
        comp, zs = place(q)
        return pltpu.make_async_copy(xpen.at[q], g_ref.at[comp, 2, :, :, zs], own_sem.at[6, q])

    def start(family, q):
        others, own = family(q)
        for copy in others:
            copy.start()
        own.start()

    def arrived(family, q):
        others, own = family(q)
        for copy in others:
            copy.wait_recv()
        own.wait()

    def sent(family, q):
        for copy in family(q)[0]:
            copy.wait_send()

    def flat(x, width):
        if yc % 16:
            return x.astype(jnp.float32).reshape(-1, width).astype(x.dtype)
        return x.reshape(-1, width)

    def cast(q):
        @pl.loop(0, zh)
        def _(z):
            for part in range(k):
                for w in range(rows):
                    field = stage[q % 2, z, pl.ds(part * yc, yc), pl.ds(w * xb, xb)]
                    blocks[q, w, part, z] = field.astype(blocks.dtype)

    def along_y(q):
        @pl.loop(0, zh)
        def _(z):
            field = flat(ypen[q, :, :, z], xb)
            product = jnp.dot(yop[...], field, preferred_element_type=jnp.float32)
            ay[q, :, :, z] = product.reshape(rows, k, yc, xb).astype(ay.dtype)

    def along_x(q):
        field = jnp.concatenate([flat(xpen[q, j], xb) for j in range(rows)], axis=1)

        @pl.loop(0, rows)
        def _(w):
            operator = xop[:, pl.ds(pl.multiple_of(w * xb, 128), xb)]
            product = jnp.dot(field, operator, preferred_element_type=jnp.float32)
            blocks[q, w] = product.reshape(k, zh, yc, xb).astype(blocks.dtype)

    def z_of(n):
        half, block = n // (nz // parts * group), n // (zh * group) % cols
        return block * zb + half * zh + n // group % zh

    def make_kron():
        wide = nz // parts * group
        tall = wide

        @pl.loop(0, parts)
        def _(m):
            at = lax.broadcasted_iota(jnp.int32, (tall, nz), 0) + m * tall
            pick = jnp.where(z_of(at) == lax.broadcasted_iota(jnp.int32, (tall, nz), 1), 1.0, 0.0)
            line = lax.dot_general(
                pick.astype(kron.dtype), zop_ref[...].astype(kron.dtype), (((1,), (1,)), ((), ())),
                preferred_element_type=jnp.float32,
            ).astype(kron.dtype)
            for h in range(parts):
                across = lax.broadcasted_iota(jnp.int32, (nz, wide), 1) + h * wide
                spread = jnp.where(z_of(across) == lax.broadcasted_iota(jnp.int32, (nz, wide), 0), 1.0, 0.0)
                full = jnp.dot(line, spread.astype(kron.dtype), preferred_element_type=jnp.float32)
                down = lax.broadcasted_iota(jnp.int32, (tall, wide), 0) % group
                same = down == lax.broadcasted_iota(jnp.int32, (tall, wide), 1) % group
                kron[h, pl.ds(m * tall, tall)] = jnp.where(same, full, 0.0).astype(kron.dtype)

    def along_z(comp):
        tall = nz // parts * group

        @pl.loop(0, parts)
        def _(m):
            lines = []
            for g in range(yc // group):
                total = None
                for h in range(parts):
                    if yc % 16:
                        field = ypen[comp * parts + h].astype(jnp.float32)[:, :, :, g * group:(g + 1) * group]
                    else:
                        field = ypen[comp * parts + h, :, :, :, pl.ds(g * group, group)]
                    field = field.reshape(-1, xb).astype(kron.dtype)
                    part = jnp.dot(kron[h, pl.ds(m * tall, tall)], field, preferred_element_type=jnp.float32)
                    total = part if total is None else total + part
                lines.append(total.reshape(rows, k, zh, group, xb))
            q = comp * parts + m
            if yc % 16:
                xpen[q] = jnp.concatenate(lines, axis=3).astype(xpen.dtype)
            else:
                for g, line in enumerate(lines):
                    xpen[q, :, :, :, pl.ds(g * group, group)] = line.astype(xpen.dtype)

    def pass_on(q):
        arrived(row_v, q)
        start(col_v, q)

    @pl.loop(0, chunks)
    def _(q):
        load(q).wait()
        cast(q)
        start(row_v, q)

        @pl.when(q + 2 < chunks)
        def _():
            load(q + 2).start()

        @pl.when(q > 0)
        def _():
            pass_on(q - 1)

    pass_on(chunks - 1)
    for copy in load_operators():
        copy.wait()
    yop[...] = (yop_in[...] * metric_ref[...]).T.astype(yop.dtype)

    @pl.loop(0, rows)
    def _(w):
        lines = pl.ds(w * xb, xb)
        xop[lines] = xop_in[lines].astype(xop.dtype)

    @pl.loop(0, chunks)
    def _(q):
        along_y(q)

    make_kron()

    def finish_x(q):
        sent(row_v, q)
        arrived(row_f, q)
        along_x(q)
        start(row_x, q)

    @pl.loop(0, chunks)
    def _(q):
        arrived(col_v, q)
        start(row_f, q)
        start(col_y, q)

        @pl.when(q > 0)
        def _():
            finish_x(q - 1)

    finish_x(chunks - 1)

    @pl.loop(0, chunks)
    def _(q):
        sent(col_v, q)
        field_in(q).start()

    @pl.loop(0, chunks // parts)
    def _(comp):
        for h in range(parts):
            field_in(comp * parts + h).wait()
        along_z(comp)
        for h in range(parts):
            along_z_out(comp * parts + h).start()

    @pl.loop(0, chunks)
    def _(q):
        arrived(row_x, q)
        arrived(col_y, q)
        along_z_out(q).wait()
        for family in (col_y, row_f, row_x):
            sent(family, q)


def shards(rows, cols, velocity, x_operator, y_operator, z_operator, y_metric):
    bf16 = jnp.bfloat16
    comps, zb, yb, nx = velocity.shape
    k = cols // rows
    yc, xb, ny, nz = yb // k, nx // rows, yb * rows, zb * cols
    parts = PARTS
    zh, chunks = zb // parts, comps * parts
    group = 16 if yc % 16 == 0 else 8

    buffer = pltpu.VMEM((chunks, rows, k, zh, yc, xb), bf16)
    row_sem = pltpu.SemaphoreType.DMA((chunks, rows - 1))
    col_sem = pltpu.SemaphoreType.DMA((chunks, cols - 1))
    work = comps * zb * yb * nx
    _, grads = pl.pallas_call(
        functools.partial(kernel, rows, cols, parts),
        out_shape=[
            jax.ShapeDtypeStruct((comps, rows, k, zb, yc, xb), bf16),
            jax.ShapeDtypeStruct((comps, 3, rows, k, zb, yc, xb), bf16),
        ],
        in_specs=[pl.BlockSpec(memory_space=pl.ANY)] * 3 + [pl.BlockSpec(memory_space=pltpu.VMEM)] * 2,
        out_specs=[pl.BlockSpec(memory_space=pl.ANY)] * 2,
        scratch_shapes=[
            buffer, buffer, buffer, buffer,
            pltpu.VMEM((2, zh, yb, nx), jnp.float32),
            pltpu.VMEM((nx, nx), jnp.float32),
            pltpu.VMEM((ny, ny), jnp.float32),
            pltpu.VMEM((nx, nx), bf16),
            pltpu.VMEM((ny, ny), bf16),
            pltpu.VMEM((parts, nz * group, nz // parts * group), bf16),
            row_sem, row_sem, col_sem, col_sem, col_sem, col_sem, row_sem, row_sem, row_sem, row_sem,
            pltpu.SemaphoreType.DMA((7, chunks)),
            pltpu.SemaphoreType.DMA((4,)),
        ],
        cost_estimate=pl.CostEstimate(
            flops=2 * work * (nx + ny + nz * group), bytes_accessed=14 * work, transcendentals=0
        ),
        compiler_params=pltpu.CompilerParams(
            collective_id=0, has_side_effects=True, vmem_limit_bytes=61 * 2**20
        ),
    )(velocity, x_operator, y_operator, y_metric[None, :], z_operator)
    return grads.reshape(3 * comps, nz, yc, xb)


def solution(mesh):
    return jax.shard_map(
        functools.partial(shards, mesh.shape["row"], mesh.shape["col"]),
        mesh=mesh,
        in_specs=(P(None, "col", "row", None), P(), P(), P(), P()),
        out_specs=P(None, None, "col", "row"),
        check_vma=False,
    )
```

```python
import functools

import jax
import jax.numpy as jnp
from jax import lax
from jax.experimental import pallas as pl
from jax.experimental.pallas import tpu as pltpu
from jax.sharding import PartitionSpec as P

MESH = pl.DeviceIdType.MESH
PARTS = 4
AHEAD = 3


def kernel(
    rows, cols, parts, v_ref, xop_ref, yop_ref, metric_ref, zop_ref, vz_ref, g_ref,
    ypen, ay, xpen, blocks, stage, xop_in, yop_in, xop, yop, kron,
    row_v_s, row_v_r, col_v_s, col_v_r, col_y_s, col_y_r, row_f_s, row_f_r, row_x_s, row_x_r, own_sem, stage_sem,
):
    r, c = lax.axis_index("row"), lax.axis_index("col")
    chunks, _, k, zh, yc, xb = ypen.shape
    zb, nz = zh * parts, zh * parts * cols
    group = 16 if yc % 16 == 0 else 8

    def place(q):
        return q // parts, pl.ds((q % parts) * zh, zh)

    def load(q):
        comp, zs = place(q)
        return pltpu.make_async_copy(v_ref.at[comp, zs], stage.at[q % 2], stage_sem.at[q % 2])

    def load_operators():
        return [
            pltpu.make_async_copy(yop_ref, yop_in, stage_sem.at[2]),
            pltpu.make_async_copy(xop_ref, xop_in, stage_sem.at[3]),
        ]

    load(0).start()
    load(1).start()
    for copy in load_operators():
        copy.start()

    barrier = pltpu.get_barrier_semaphore()
    for d in range(1, rows):
        pl.semaphore_signal(barrier, inc=1, device_id=(lax.rem(r + d, rows), c), device_id_type=MESH)
    for d in range(1, cols):
        pl.semaphore_signal(barrier, inc=1, device_id=(r, lax.rem(c + d, cols)), device_id_type=MESH)
    pl.semaphore_wait(barrier, rows + cols - 2)

    def remote(src, dst, send, recv, target):
        return pltpu.make_async_remote_copy(
            src_ref=src, dst_ref=dst, send_sem=send, recv_sem=recv, device_id=target, device_id_type=MESH
        )

    def row_family(q, source, dst, send, recv, own):
        others = []
        for d in range(1, rows):
            t = lax.rem(r + d, rows)
            others.append(remote(source(t), dst, send.at[q, d - 1], recv.at[q, d - 1], (t, c)))
        return others, pltpu.make_async_copy(source(r), dst, own_sem.at[own, q])

    def col_family(q, source, dst, send, recv, own):
        others = []
        for d in range(1, cols):
            t = lax.rem(c + d, cols)
            others.append(remote(source(t), dst, send.at[q, d - 1], recv.at[q, d - 1], (r, t)))
        return others, pltpu.make_async_copy(source(c), dst, own_sem.at[own, q])

    def row_v(q):
        return row_family(q, lambda t: blocks.at[q, t], ypen.at[q, r], row_v_s, row_v_r, 0)

    def col_v(q):
        comp, zs = place(q)
        dst = vz_ref.at[comp, c // k, c % k, zs]
        return col_family(q, lambda t: ypen.at[q, t // k, t % k], dst, col_v_s, col_v_r, 1)

    def col_y(q):
        comp, zs = place(q)
        dst = g_ref.at[comp, 1, c // k, c % k, zs]
        return col_family(q, lambda t: ay.at[q, t // k, t % k], dst, col_y_s, col_y_r, 2)

    def row_f(q):
        comp, zs = place(q)
        return row_family(q, lambda t: vz_ref.at[comp, t, :, zs], xpen.at[q, r], row_f_s, row_f_r, 3)

    def row_x(q):
        comp, zs = place(q)
        return row_family(q, lambda t: blocks.at[q, t], g_ref.at[comp, 0, r, :, zs], row_x_s, row_x_r, 4)

    def field_in(q):
        comp, zs = place(q)
        return pltpu.make_async_copy(vz_ref.at[comp, :, :, zs], ypen.at[q], own_sem.at[5, q])

    def along_z_out(q):
        comp, zs = place(q)
        return pltpu.make_async_copy(xpen.at[q], g_ref.at[comp, 2, :, :, zs], own_sem.at[6, q])

    def start(family, q):
        others, own = family(q)
        for copy in others:
            copy.start()
        own.start()

    def arrived(family, q):
        others, own = family(q)
        for copy in others:
            copy.wait_recv()
        own.wait()

    def sent(family, q):
        for copy in family(q)[0]:
            copy.wait_send()

    def flat(x, width):
        if yc % 16:
            return x.astype(jnp.float32).reshape(-1, width).astype(x.dtype)
        return x.reshape(-1, width)

    def cast(q):
        @pl.loop(0, zh)
        def _(z):
            for part in range(k):
                for w in range(rows):
                    field = stage[q % 2, z, pl.ds(part * yc, yc), pl.ds(w * xb, xb)]
                    blocks[q, w, part, z] = field.astype(blocks.dtype)

    def along_y(q):
        @pl.loop(0, zh)
        def _(z):
            field = flat(ypen[q, :, :, z], xb)
            product = jnp.dot(yop[...], field, preferred_element_type=jnp.float32)
            ay[q, :, :, z] = product.reshape(rows, k, yc, xb).astype(ay.dtype)

    def along_x(q):
        field = jnp.concatenate([flat(xpen[q, j], xb) for j in range(rows)], axis=1)

        @pl.loop(0, rows)
        def _(w):
            operator = xop[:, pl.ds(pl.multiple_of(w * xb, 128), xb)]
            product = jnp.dot(field, operator, preferred_element_type=jnp.float32)
            blocks[q, w] = product.reshape(k, zh, yc, xb).astype(blocks.dtype)

    def z_of(n):
        half, block = n // (nz // parts * group), n // (zh * group) % cols
        return block * zb + half * zh + n // group % zh

    def make_kron():
        wide = nz // parts * group
        tall = wide

        @pl.loop(0, parts)
        def _(m):
            at = lax.broadcasted_iota(jnp.int32, (tall, nz), 0) + m * tall
            pick = jnp.where(z_of(at) == lax.broadcasted_iota(jnp.int32, (tall, nz), 1), 1.0, 0.0)
            line = lax.dot_general(
                pick.astype(kron.dtype), zop_ref[...].astype(kron.dtype), (((1,), (1,)), ((), ())),
                preferred_element_type=jnp.float32,
            ).astype(kron.dtype)
            for h in range(parts):
                across = lax.broadcasted_iota(jnp.int32, (nz, wide), 1) + h * wide
                spread = jnp.where(z_of(across) == lax.broadcasted_iota(jnp.int32, (nz, wide), 0), 1.0, 0.0)
                full = jnp.dot(line, spread.astype(kron.dtype), preferred_element_type=jnp.float32)
                down = lax.broadcasted_iota(jnp.int32, (tall, wide), 0) % group
                same = down == lax.broadcasted_iota(jnp.int32, (tall, wide), 1) % group
                kron[h, pl.ds(m * tall, tall)] = jnp.where(same, full, 0.0).astype(kron.dtype)

    def along_z(comp):
        tall = nz // parts * group

        @pl.loop(0, parts)
        def _(m):
            lines = []
            for g in range(yc // group):
                total = None
                for h in range(parts):
                    if yc % 16:
                        field = ypen[comp * parts + h].astype(jnp.float32)[:, :, :, g * group:(g + 1) * group]
                    else:
                        field = ypen[comp * parts + h, :, :, :, pl.ds(g * group, group)]
                    field = field.reshape(-1, xb).astype(kron.dtype)
                    part = jnp.dot(kron[h, pl.ds(m * tall, tall)], field, preferred_element_type=jnp.float32)
                    total = part if total is None else total + part
                lines.append(total.reshape(rows, k, zh, group, xb))
            q = comp * parts + m
            if yc % 16:
                xpen[q] = jnp.concatenate(lines, axis=3).astype(xpen.dtype)
            else:
                for g, line in enumerate(lines):
                    xpen[q, :, :, :, pl.ds(g * group, group)] = line.astype(xpen.dtype)

    def pass_on(q):
        arrived(row_v, q)
        start(col_v, q)

    def begin(q):
        load(q).wait()
        cast(q)
        start(row_v, q)

        @pl.when(q + 2 < chunks)
        def _():
            load(q + 2).start()

    def finish_x(q):
        sent(row_v, q)
        arrived(row_f, q)
        along_x(q)
        start(row_x, q)

    @pl.loop(0, AHEAD + 1)
    def _(q):
        begin(q)

        @pl.when(q > 0)
        def _():
            pass_on(q - 1)

    for copy in load_operators():
        copy.wait()
    yop[...] = (yop_in[...] * metric_ref[...][None, :]).T.astype(yop.dtype)

    @pl.loop(0, rows)
    def _(w):
        lines = pl.ds(w * xb, xb)
        xop[lines] = xop_in[lines].astype(xop.dtype)

    make_kron()

    @pl.loop(0, chunks)
    def _(q):
        @pl.when(q + AHEAD + 1 < chunks)
        def _():
            begin(q + AHEAD + 1)

        arrived(col_v, q)

        @pl.when(q + AHEAD < chunks)
        def _():
            pass_on(q + AHEAD)

        start(row_f, q)
        along_y(q)

        @pl.when(q + AHEAD >= chunks)
        def _():
            start(col_y, q + AHEAD - chunks)

        @pl.when(q >= 2)
        def _():
            finish_x(q - 2)

    @pl.loop(AHEAD, chunks)
    def _(q):
        start(col_y, q)

    finish_x(chunks - 2)
    finish_x(chunks - 1)

    @pl.loop(0, chunks)
    def _(q):
        sent(col_v, q)
        field_in(q).start()

    @pl.loop(0, chunks // parts)
    def _(comp):
        for h in range(parts):
            field_in(comp * parts + h).wait()
        along_z(comp)
        for h in range(parts):
            along_z_out(comp * parts + h).start()

    @pl.loop(0, chunks)
    def _(q):
        arrived(row_x, q)
        arrived(col_y, q)
        along_z_out(q).wait()
        for family in (col_y, row_f, row_x):
            sent(family, q)


def shards(rows, cols, velocity, x_operator, y_operator, z_operator, y_metric):
    bf16 = jnp.bfloat16
    comps, zb, yb, nx = velocity.shape
    k = cols // rows
    yc, xb, ny, nz = yb // k, nx // rows, yb * rows, zb * cols
    parts = PARTS
    zh, chunks = zb // parts, comps * parts
    group = 16 if yc % 16 == 0 else 8

    buffer = pltpu.VMEM((chunks, rows, k, zh, yc, xb), bf16)
    row_sem = pltpu.SemaphoreType.DMA((chunks, rows - 1))
    col_sem = pltpu.SemaphoreType.DMA((chunks, cols - 1))
    work = comps * zb * yb * nx
    _, grads = pl.pallas_call(
        functools.partial(kernel, rows, cols, parts),
        out_shape=[
            jax.ShapeDtypeStruct((comps, rows, k, zb, yc, xb), bf16),
            jax.ShapeDtypeStruct((comps, 3, rows, k, zb, yc, xb), bf16),
        ],
        in_specs=[pl.BlockSpec(memory_space=pl.ANY)] * 3 + [pl.BlockSpec(memory_space=pltpu.VMEM)] * 2,
        out_specs=[pl.BlockSpec(memory_space=pl.ANY)] * 2,
        scratch_shapes=[
            buffer, buffer, buffer, buffer,
            pltpu.VMEM((2, zh, yb, nx), jnp.float32),
            pltpu.VMEM((nx, nx), jnp.float32),
            pltpu.VMEM((ny, ny), jnp.float32),
            pltpu.VMEM((nx, nx), bf16),
            pltpu.VMEM((ny, ny), bf16),
            pltpu.VMEM((parts, nz * group, nz // parts * group), bf16),
            row_sem, row_sem, col_sem, col_sem, col_sem, col_sem, row_sem, row_sem, row_sem, row_sem,
            pltpu.SemaphoreType.DMA((7, chunks)),
            pltpu.SemaphoreType.DMA((4,)),
        ],
        cost_estimate=pl.CostEstimate(
            flops=2 * work * (nx + ny + nz * group), bytes_accessed=14 * work, transcendentals=0
        ),
        compiler_params=pltpu.CompilerParams(
            collective_id=0, has_side_effects=True, vmem_limit_bytes=61 * 2**20
        ),
    )(velocity, x_operator, y_operator, y_metric, z_operator)
    return grads.reshape(3 * comps, nz, yc, xb)


def solution(mesh):
    return jax.shard_map(
        functools.partial(shards, mesh.shape["row"], mesh.shape["col"]),
        mesh=mesh,
        in_specs=(P(None, "col", "row", None), P(), P(), P(), P()),
        out_specs=P(None, None, "col", "row"),
        check_vma=False,
    )
```

```python
import functools

import jax
import jax.numpy as jnp
from jax import lax
from jax.experimental import pallas as pl
from jax.experimental.pallas import tpu as pltpu
from jax.sharding import PartitionSpec as P

MESH = pl.DeviceIdType.MESH
PARTS = 4


def kernel(
    rows, cols, parts, v_ref, xop_ref, yop_ref, metric_ref, zop_ref, vz_ref, g_ref,
    ypen, ay, xpen, blocks, stage, xop_in, yop_in, xop, yop, kron,
    row_v_s, row_v_r, col_v_s, col_v_r, col_y_s, col_y_r, row_f_s, row_f_r, row_x_s, row_x_r, own_sem, stage_sem,
):
    r, c = lax.axis_index("row"), lax.axis_index("col")
    chunks, _, k, zh, yc, xb = ypen.shape
    zb, nz = zh * parts, zh * parts * cols
    group = 16 if yc % 16 == 0 else 8

    def place(q):
        return q // parts, pl.ds((q % parts) * zh, zh)

    def load(q):
        comp, zs = place(q)
        return pltpu.make_async_copy(v_ref.at[comp, zs], stage.at[q % 2], stage_sem.at[q % 2])

    def load_operators():
        return [
            pltpu.make_async_copy(yop_ref, yop_in, stage_sem.at[2]),
            pltpu.make_async_copy(xop_ref, xop_in, stage_sem.at[3]),
        ]

    load(0).start()
    load(1).start()
    for copy in load_operators():
        copy.start()

    barrier = pltpu.get_barrier_semaphore()
    for d in range(1, rows):
        pl.semaphore_signal(barrier, inc=1, device_id=(lax.rem(r + d, rows), c), device_id_type=MESH)
    for d in range(1, cols):
        pl.semaphore_signal(barrier, inc=1, device_id=(r, lax.rem(c + d, cols)), device_id_type=MESH)
    pl.semaphore_wait(barrier, rows + cols - 2)

    def remote(src, dst, send, recv, target):
        return pltpu.make_async_remote_copy(
            src_ref=src, dst_ref=dst, send_sem=send, recv_sem=recv, device_id=target, device_id_type=MESH
        )

    def row_family(q, source, dst, send, recv, own):
        others = []
        for d in range(1, rows):
            t = lax.rem(r + d, rows)
            others.append(remote(source(t), dst, send.at[q, d - 1], recv.at[q, d - 1], (t, c)))
        return others, pltpu.make_async_copy(source(r), dst, own_sem.at[own, q])

    far_first = sorted(range(1, cols), key=lambda d: abs(d - cols // 2))
    col_order = []
    while far_first:
        col_order.append(far_first.pop(0))
        if far_first:
            col_order.append(far_first.pop())

    def col_family(q, source, dst, send, recv, own):
        others = []
        for d in col_order:
            t = lax.rem(c + d, cols)
            others.append(remote(source(t), dst, send.at[q, d - 1], recv.at[q, d - 1], (r, t)))
        return others, pltpu.make_async_copy(source(c), dst, own_sem.at[own, q])

    def row_v(q):
        return row_family(q, lambda t: blocks.at[q, t], ypen.at[q, r], row_v_s, row_v_r, 0)

    def col_v(q):
        comp, zs = place(q)
        dst = vz_ref.at[comp, c // k, c % k, zs]
        return col_family(q, lambda t: ypen.at[q, t // k, t % k], dst, col_v_s, col_v_r, 1)

    def col_y(q):
        comp, zs = place(q)
        dst = g_ref.at[comp, 1, c // k, c % k, zs]
        return col_family(q, lambda t: ay.at[q, t // k, t % k], dst, col_y_s, col_y_r, 2)

    def row_f(q):
        comp, zs = place(q)
        return row_family(q, lambda t: vz_ref.at[comp, t, :, zs], xpen.at[q, r], row_f_s, row_f_r, 3)

    def row_x(q):
        comp, zs = place(q)
        return row_family(q, lambda t: blocks.at[q, t], g_ref.at[comp, 0, r, :, zs], row_x_s, row_x_r, 4)

    def field_in(q):
        comp, zs = place(q)
        return pltpu.make_async_copy(vz_ref.at[comp, :, :, zs], ypen.at[q], own_sem.at[5, q])

    def along_z_out(q):
        comp, zs = place(q)
        return pltpu.make_async_copy(xpen.at[q], g_ref.at[comp, 2, :, :, zs], own_sem.at[6, q])

    def start(family, q):
        others, own = family(q)
        for copy in others:
            copy.start()
        own.start()

    def arrived(family, q):
        others, own = family(q)
        for copy in others:
            copy.wait_recv()
        own.wait()

    def sent(family, q):
        for copy in family(q)[0]:
            copy.wait_send()

    def flat(x, width):
        if yc % 16:
            return x.astype(jnp.float32).reshape(-1, width).astype(x.dtype)
        return x.reshape(-1, width)

    def cast(q):
        @pl.loop(0, zh)
        def _(z):
            for part in range(k):
                for w in range(rows):
                    field = stage[q % 2, z, pl.ds(part * yc, yc), pl.ds(w * xb, xb)]
                    blocks[q, w, part, z] = field.astype(blocks.dtype)

    def along_y(q):
        @pl.loop(0, zh)
        def _(z):
            field = flat(ypen[q, :, :, z], xb)
            product = jnp.dot(yop[...], field, preferred_element_type=jnp.float32)
            ay[q, :, :, z] = product.reshape(rows, k, yc, xb).astype(ay.dtype)

    def along_x(q):
        field = jnp.concatenate([flat(xpen[q, j], xb) for j in range(rows)], axis=1)

        @pl.loop(0, rows)
        def _(w):
            operator = xop[:, pl.ds(pl.multiple_of(w * xb, 128), xb)]
            product = jnp.dot(field, operator, preferred_element_type=jnp.float32)
            blocks[q, w] = product.reshape(k, zh, yc, xb).astype(blocks.dtype)

    def z_of(n):
        half, block = n // (nz // parts * group), n // (zh * group) % cols
        return block * zb + half * zh + n // group % zh

    def make_kron():
        wide = nz // parts * group
        tall = wide

        @pl.loop(0, parts)
        def _(m):
            at = lax.broadcasted_iota(jnp.int32, (tall, nz), 0) + m * tall
            pick = jnp.where(z_of(at) == lax.broadcasted_iota(jnp.int32, (tall, nz), 1), 1.0, 0.0)
            line = lax.dot_general(
                pick.astype(kron.dtype), zop_ref[...].astype(kron.dtype), (((1,), (1,)), ((), ())),
                preferred_element_type=jnp.float32,
            ).astype(kron.dtype)
            for h in range(parts):
                across = lax.broadcasted_iota(jnp.int32, (nz, wide), 1) + h * wide
                spread = jnp.where(z_of(across) == lax.broadcasted_iota(jnp.int32, (nz, wide), 0), 1.0, 0.0)
                full = jnp.dot(line, spread.astype(kron.dtype), preferred_element_type=jnp.float32)
                down = lax.broadcasted_iota(jnp.int32, (tall, wide), 0) % group
                same = down == lax.broadcasted_iota(jnp.int32, (tall, wide), 1) % group
                kron[h, pl.ds(m * tall, tall)] = jnp.where(same, full, 0.0).astype(kron.dtype)

    def along_z(comp):
        tall = nz // parts * group

        @pl.loop(0, parts)
        def _(m):
            lines = []
            for g in range(yc // group):
                total = None
                for h in range(parts):
                    if yc % 16:
                        field = ypen[comp * parts + h].astype(jnp.float32)[:, :, :, g * group:(g + 1) * group]
                    else:
                        field = ypen[comp * parts + h, :, :, :, pl.ds(g * group, group)]
                    field = field.reshape(-1, xb).astype(kron.dtype)
                    part = jnp.dot(kron[h, pl.ds(m * tall, tall)], field, preferred_element_type=jnp.float32)
                    total = part if total is None else total + part
                lines.append(total.reshape(rows, k, zh, group, xb))
            q = comp * parts + m
            if yc % 16:
                xpen[q] = jnp.concatenate(lines, axis=3).astype(xpen.dtype)
            else:
                for g, line in enumerate(lines):
                    xpen[q, :, :, :, pl.ds(g * group, group)] = line.astype(xpen.dtype)

    def pass_on(q):
        arrived(row_v, q)
        start(col_v, q)

    @pl.loop(0, chunks)
    def _(q):
        load(q).wait()
        cast(q)
        start(row_v, q)

        @pl.when(q + 2 < chunks)
        def _():
            load(q + 2).start()

        @pl.when(q > 0)
        def _():
            pass_on(q - 1)

    pass_on(chunks - 1)
    for copy in load_operators():
        copy.wait()
    yop[...] = (yop_in[...] * metric_ref[...][None, :]).T.astype(yop.dtype)

    @pl.loop(0, rows)
    def _(w):
        lines = pl.ds(w * xb, xb)
        xop[lines] = xop_in[lines].astype(xop.dtype)

    @pl.loop(0, chunks)
    def _(q):
        along_y(q)

    make_kron()

    def finish_x(q):
        sent(row_v, q)
        arrived(row_f, q)
        along_x(q)
        start(row_x, q)

    @pl.loop(0, chunks)
    def _(q):
        arrived(col_v, q)
        start(row_f, q)
        start(col_y, q)

        @pl.when(q > 0)
        def _():
            finish_x(q - 1)

    finish_x(chunks - 1)

    @pl.loop(0, chunks)
    def _(q):
        sent(col_v, q)
        field_in(q).start()

    @pl.loop(0, chunks // parts)
    def _(comp):
        for h in range(parts):
            field_in(comp * parts + h).wait()
        along_z(comp)
        for h in range(parts):
            along_z_out(comp * parts + h).start()

    @pl.loop(0, chunks)
    def _(q):
        arrived(row_x, q)
        arrived(col_y, q)
        along_z_out(q).wait()
        for family in (col_y, row_f, row_x):
            sent(family, q)


def shards(rows, cols, velocity, x_operator, y_operator, z_operator, y_metric):
    bf16 = jnp.bfloat16
    comps, zb, yb, nx = velocity.shape
    k = cols // rows
    yc, xb, ny, nz = yb // k, nx // rows, yb * rows, zb * cols
    parts = PARTS
    zh, chunks = zb // parts, comps * parts
    group = 16 if yc % 16 == 0 else 8

    buffer = pltpu.VMEM((chunks, rows, k, zh, yc, xb), bf16)
    row_sem = pltpu.SemaphoreType.DMA((chunks, rows - 1))
    col_sem = pltpu.SemaphoreType.DMA((chunks, cols - 1))
    work = comps * zb * yb * nx
    _, grads = pl.pallas_call(
        functools.partial(kernel, rows, cols, parts),
        out_shape=[
            jax.ShapeDtypeStruct((comps, rows, k, zb, yc, xb), bf16),
            jax.ShapeDtypeStruct((comps, 3, rows, k, zb, yc, xb), bf16),
        ],
        in_specs=[pl.BlockSpec(memory_space=pl.ANY)] * 3 + [pl.BlockSpec(memory_space=pltpu.VMEM)] * 2,
        out_specs=[pl.BlockSpec(memory_space=pl.ANY)] * 2,
        scratch_shapes=[
            buffer, buffer, buffer, buffer,
            pltpu.VMEM((2, zh, yb, nx), jnp.float32),
            pltpu.VMEM((nx, nx), jnp.float32),
            pltpu.VMEM((ny, ny), jnp.float32),
            pltpu.VMEM((nx, nx), bf16),
            pltpu.VMEM((ny, ny), bf16),
            pltpu.VMEM((parts, nz * group, nz // parts * group), bf16),
            row_sem, row_sem, col_sem, col_sem, col_sem, col_sem, row_sem, row_sem, row_sem, row_sem,
            pltpu.SemaphoreType.DMA((7, chunks)),
            pltpu.SemaphoreType.DMA((4,)),
        ],
        cost_estimate=pl.CostEstimate(
            flops=2 * work * (nx + ny + nz * group), bytes_accessed=14 * work, transcendentals=0
        ),
        compiler_params=pltpu.CompilerParams(
            collective_id=0, has_side_effects=True, vmem_limit_bytes=61 * 2**20
        ),
    )(velocity, x_operator, y_operator, y_metric, z_operator)
    return grads.reshape(3 * comps, nz, yc, xb)


def solution(mesh):
    return jax.shard_map(
        functools.partial(shards, mesh.shape["row"], mesh.shape["col"]),
        mesh=mesh,
        in_specs=(P(None, "col", "row", None), P(), P(), P(), P()),
        out_specs=P(None, None, "col", "row"),
        check_vma=False,
    )
```
